256 devices in a mesh: wide: 64 (over y, z, core), narrow: 4 (over x).
Axes of the slice: x: 4, y: 4, z: 8, core: 2. Of those that a mesh axis runs over, the one named last changes fastest.
Arguments:
- acts: bfloat16 [1024, 8192], P(None, 'wide'), may hold values from -6 to 6
- grads: bfloat16 [1024, 28672], P('wide', 'narrow'), may hold values from -6 to 6
- act_basis: bfloat16 [8192, 8192], P('wide', 'narrow'), may hold values from -0.0625 to 0.0625
- grad_basis: bfloat16 [28672, 28672], P('narrow', 'wide'), may hold values from -0.03125 to 0.03125
Outputs:
- eigenvalues: float32 [28672, 8192], P('wide', 'narrow')
The draws below stay inside these ranges and needn't reach their ends.
All inputs are finite; a program needn't handle non-finite values.
Results may differ from the reference program's by a relative error of at most 0.0027.
Values may be sent and summed in bfloat16 or wider, within the bound.
No kernel may reach another device: no remote copies, remote signals or barrier semaphores. Data moves between devices by JAX's collectives and lax.ppermute only.
A program may use at most 128 MiB of HBM per device.

```python
import jax
import jax.numpy as jnp
from jax import lax

D_IN = 8192
D_OUT = 28672
EXAMPLES = 8
T_EX = 128
TOKENS = 1024


def levels(rng, shape, cuts, low, largest):
    factor_of = 1.0
    for axis_at, shards_of in cuts:
        heights = jax.random.uniform(jax.random.fold_in(jax.random.fold_in(rng, 6), axis_at), (shards_of,), jnp.float32, low / len(cuts), largest / len(cuts))
        factor_of = factor_of * jnp.repeat(jnp.exp(heights), shape[axis_at] // shards_of).reshape((-1,) + (1,) * (len(shape) - 1 - axis_at))
    return factor_of


def normal_values(key, extent, scale, limit, cuts=(), kind=jnp.bfloat16):
    loudness = levels(key, extent, cuts, -0.22, 0.18) if cuts else 1.0
    result = jax.random.normal(key, extent, jnp.float32) * scale * loudness
    return jnp.minimum(jnp.maximum(result, -limit), limit).astype(kind)


def setup_inputs(seed: int = 0) -> dict:
    keys = jax.random.split(jax.random.key(seed), 5)
    acts = normal_values(keys[0], (TOKENS, D_IN), 1.0, 6.0, ((1, 64),))
    grads = normal_values(keys[1], (TOKENS, D_OUT), 1.0, 6.0, ((0, 64), (1, 4)))
    act_basis = normal_values(keys[2], (D_IN, D_IN), D_IN ** -0.5, 0.0625, ((0, 64), (1, 4)))
    grad_basis = normal_values(keys[3], (D_OUT, D_OUT), D_OUT ** -0.5, 0.03125, ((0, 4), (1, 64)))
    return dict(acts=acts, grads=grads, act_basis=act_basis, grad_basis=grad_basis)


def reference(acts, grads, act_basis, grad_basis):
    rot_grads = jnp.dot(grads, grad_basis, preferred_element_type=jnp.float32).astype(jnp.bfloat16)
    rot_acts = jnp.dot(acts, act_basis, preferred_element_type=jnp.float32).astype(jnp.bfloat16)
    grads_ex = rot_grads.reshape(EXAMPLES, T_EX, D_OUT)
    acts_ex = rot_acts.reshape(EXAMPLES, T_EX, D_IN)

    def accumulate(total, pair):
        rotated = jnp.dot(pair[0].T, pair[1], preferred_element_type=jnp.float32)
        return total + rotated * rotated, None

    start = jnp.zeros((D_OUT, D_IN), jnp.float32)
    total, unused = lax.scan(accumulate, start, (grads_ex, acts_ex))
    return total / (EXAMPLES * T_EX)
```

```python
import jax
import jax.numpy as jnp
import numpy as np
from jax import lax
from jax.experimental import pallas as pl
from jax.experimental.pallas import tpu as pltpu
from jax.sharding import PartitionSpec as P

EXAMPLES = 8
T_EX = 128
NY, NZ, NC, NX = 4, 8, 2, 4
ROWS = 16
GROUPS = ((0,), (1, 7), (2, 6), (3, 5), (4,))
Y_STEPS = (0, -1, 1, 2)
BF16, F32 = jnp.bfloat16, jnp.float32


def shift(v, dy=0, dz=0, dc=0):
    def at(y, z, c):
        return ((y % NY) * NZ + z % NZ) * NC + c % NC

    pairs = [(at(y, z, c), at(y + dy, z + dz, c + dc)) for y in range(NY) for z in range(NZ) for c in range(NC)]
    return lax.ppermute(v, "wide", pairs)


def shift_x(v, d):
    return lax.ppermute(v, "narrow", [(i, (i + d) % NX) for i in range(NX)])


def ring_z(v):
    up, down = [v], [v]
    for _ in range(4):
        up.append(shift(up[-1], dz=1))
    for _ in range(3):
        down.append(shift(down[-1], dz=-1))
    return up + down[:0:-1]


def finish_kernel(table, g_ref, own_ref, other_ref, o_ref, rows, turned):
    @pl.when(pl.program_id(0) == 0)
    def _():
        for i in range(g_ref.shape[0] // ROWS):
            at = pl.multiple_of(table[i] * ROWS, ROWS)
            rows[pl.ds(at, ROWS), :] = g_ref[i * ROWS : (i + 1) * ROWS, :]
        for e in range(EXAMPLES):
            turned[e] = rows[e * T_EX : (e + 1) * T_EX, :].T

    for i in range(EXAMPLES):
        ref = own_ref if i < NY else other_ref
        e = table[NY * NZ * NC + i]
        r = jnp.dot(turned[e], ref[0, i % NY], preferred_element_type=F32)
        r = r * r
        if i > 0:
            r = r + o_ref[...]
        if i == EXAMPLES - 1:
            r = r * (1.0 / (EXAMPLES * T_EX))
        o_ref[...] = r


def finish(table, g_all, own, other):
    tokens, cols = g_all.shape
    n_blk = own.shape[3]
    spec_a = pl.BlockSpec((1, NY, T_EX, n_blk), lambda j, t: (j, 0, 0, 0))
    return pl.pallas_call(
        finish_kernel,
        grid_spec=pltpu.PrefetchScalarGridSpec(
            num_scalar_prefetch=1,
            grid=(NZ,),
            in_specs=[pl.BlockSpec((tokens, cols), lambda j, t: (0, 0)), spec_a, spec_a],
            out_specs=pl.BlockSpec((cols, n_blk), lambda j, t: (0, t[NY * NZ * NC + EXAMPLES + j])),
            scratch_shapes=[pltpu.VMEM((tokens, cols), BF16), pltpu.VMEM((EXAMPLES, cols, T_EX), BF16)],
        ),
        out_shape=jax.ShapeDtypeStruct((cols, NZ * n_blk), F32),
        compiler_params=pltpu.CompilerParams(vmem_limit_bytes=24 * 2**20),
        cost_estimate=pl.CostEstimate(
            flops=2 * tokens * cols * NZ * n_blk, bytes_accessed=4 * cols * NZ * n_blk + 4 * tokens * n_blk * NZ, transcendentals=0
        ),
    )(table, g_all, own, other)


def places(w, x):
    c, z, y = w % NC, (w // NC) % NZ, w // (NC * NZ)
    steps = jnp.array(Y_STEPS, jnp.int32)
    out = []
    for group in GROUPS:
        for d in range(NX):
            y_at = (y + steps[(x - d) % NX]) % NY
            for s in range(NC):
                for dz in group:
                    out.append((y_at * NZ + (z - dz) % NZ) * NC + (c + s) % NC)
    for s in range(NC):
        for d in range(NY):
            r = ((c + s) % NC) * NY + (y - d) % NY
            out.append(2 * ((x - r // 2) % NX) + r % 2)
    for dz in range(NZ):
        out.append((z - dz) % NZ)
    return jnp.stack(out).astype(jnp.int32)


def rotate_acts(acts, act_basis, y, z, c, x):
    quarter = acts.shape[0] // NX
    depth, n = act_basis.shape
    n_blk = n // NZ
    mine = lax.dynamic_slice_in_dim(acts, x * quarter, quarter, 0)
    along_z = jnp.concatenate(ring_z(mine), axis=1)
    a_all = jnp.concatenate([along_z, shift_x(along_z, 1), shift_x(along_z, 2), shift_x(along_z, -1)], axis=0)
    basis = []
    for d in range(NZ):
        part = lax.dynamic_slice_in_dim(act_basis, ((z + d) % NZ) * n_blk, n_blk, 1)
        basis.append(shift(part, dz=d if d <= 4 else d - NZ) if d else part)
    partial = jnp.dot(a_all, jnp.concatenate(basis, axis=0), preferred_element_type=F32)
    halves = partial.reshape(NC, -1, n_blk)
    half = lax.dynamic_index_in_dim(halves, c, 0, False) + shift(lax.dynamic_index_in_dim(halves, 1 - c, 0, False), dc=1)
    pieces = half.reshape(NY, -1, n_blk)
    total = lax.dynamic_index_in_dim(pieces, y, 0, False)
    for d in (1, 2, -1):
        total = total + shift(lax.dynamic_index_in_dim(pieces, (y + d) % NY, 0, False), dy=d)
    piece = total.astype(BF16)
    slots = jnp.stack([piece, shift(piece, dy=1), shift(piece, dy=2), shift(piece, dy=-1)])
    own = jnp.stack(ring_z(slots))
    return own, shift(own, dc=1)


def rotate_grads(grads, grad_basis, x):
    both = jnp.concatenate([grad_basis, shift(grad_basis, dc=1)], axis=1)
    cols = grad_basis.shape[1]
    blocks = ring_z(grads)
    out = []
    for group in GROUPS:
        load = jnp.concatenate([blocks[d] for d in group], axis=0) if len(group) > 1 else blocks[group[0]]
        h = load.shape[0] // 2
        from_below, from_above = shift(load, dy=1), shift(load, dy=-1)
        far = [shift(from_below[:h], dy=1), shift(from_above[h:], dy=-1)]
        chunk = jnp.concatenate([load, from_below, from_above] + far, axis=0)
        partial = jnp.dot(chunk, both, preferred_element_type=F32).reshape(NX, 2 * h, 2 * cols)
        total = lax.dynamic_index_in_dim(partial, x, 0, False)
        for d in (1, 2, -1):
            total = total + shift_x(lax.dynamic_index_in_dim(partial, (x + d) % NX, 0, False), d)
        total = total.astype(BF16)
        piece = jnp.concatenate([total[:, :cols], shift(total[:, cols:], dc=1)], axis=0)
        out += [piece, shift_x(piece, 1), shift_x(piece, 2), shift_x(piece, -1)]
    return jnp.concatenate(out, axis=0)


def body(acts, grads, act_basis, grad_basis):
    w, x = lax.axis_index("wide"), lax.axis_index("narrow")
    c, z, y = w % NC, (w // NC) % NZ, w // (NC * NZ)
    own, other = rotate_acts(acts, act_basis, y, z, c, x)
    g_all = rotate_grads(grads, grad_basis, x)
    return finish(places(w, x), g_all, own, other)


def solution(mesh):
    return jax.shard_map(
        body,
        mesh=mesh,
        in_specs=(P(None, "wide"), P("wide", "narrow"), P("wide", "narrow"), P("narrow", "wide")),
        out_specs=P("wide", "narrow"),
        check_vma=False,
    )
```

```python
import jax
import jax.numpy as jnp
from jax import lax
from jax.experimental import pallas as pl
from jax.experimental.pallas import tpu as pltpu
from jax.sharding import Mesh, PartitionSpec as P

EXAMPLES = 8
T_EX = 128
NY, NZ, NC, NX = 4, 8, 2, 4
ROWS = 16
Y_STEPS = (0, -1, 1, 2)
BLOCKS = NY * NZ * NC
BF16, F32 = jnp.bfloat16, jnp.float32
SIZES = {"y": NY, "z": NZ, "core": NC, "x": NX}


def shift(v, axis, d):
    n = SIZES[axis]
    return lax.ppermute(v, axis, [(i, (i + d) % n) for i in range(n)])


def ring_z(v):
    up, down = [v], [v]
    for _ in range(4):
        up.append(shift(up[-1], "z", 1))
    for _ in range(3):
        down.append(shift(down[-1], "z", -1))
    return up + down[:0:-1]


def product_kernel(x_ref, b_ref, b_other_ref, o_ref, o_other_ref):
    k = pl.program_id(0)
    for b, o in ((b_ref, o_ref), (b_other_ref, o_other_ref)):
        r = lax.dot_general(x_ref[...], b[...], (((1,), (1,)), ((), ())), preferred_element_type=F32)

        @pl.when(k == 0)
        def _():
            o[...] = r

        @pl.when(k > 0)
        def _():
            o[...] += r


def product(x, b, b_other):
    rows, depth = x.shape
    cols = b.shape[0]
    step = depth // 7
    spec_b = pl.BlockSpec((cols, step), lambda k: (0, k))
    spec_o = pl.BlockSpec((rows, cols), lambda k: (0, 0))
    return pl.pallas_call(
        product_kernel,
        grid=(7,),
        in_specs=[pl.BlockSpec((rows, step), lambda k: (0, k)), spec_b, spec_b],
        out_specs=[spec_o, spec_o],
        out_shape=[jax.ShapeDtypeStruct((rows, cols), F32)] * 2,
        compiler_params=pltpu.CompilerParams(vmem_limit_bytes=24 * 2**20),
        cost_estimate=pl.CostEstimate(
            flops=4 * rows * cols * depth, bytes_accessed=2 * depth * (rows + 2 * cols) + 8 * rows * cols, transcendentals=0
        ),
    )(x, b, b_other)


def finish_kernel(table, g_ref, own_ref, other_ref, o_ref, rows, turned):
    @pl.when(pl.program_id(0) == 0)
    def _():
        for i in range(BLOCKS):
            at = pl.multiple_of(table[i] * ROWS, ROWS)
            rows[pl.ds(at, ROWS), :] = g_ref[i * ROWS : (i + 1) * ROWS, :]
        for e in range(EXAMPLES):
            turned[e] = rows[e * T_EX : (e + 1) * T_EX, :].T

    for i in range(EXAMPLES):
        ref = own_ref if i < NY else other_ref
        r = jnp.dot(turned[table[BLOCKS + i]], ref[i % NY, 0], preferred_element_type=F32)
        r = r * r
        if i > 0:
            r = r + o_ref[...]
        if i == EXAMPLES - 1:
            r = r * (1.0 / (EXAMPLES * T_EX))
        o_ref[...] = r


def finish(table, g_all, own, other):
    tokens, cols = g_all.shape
    n_blk = own.shape[3]
    spec_a = pl.BlockSpec((NY, 1, T_EX, n_blk), lambda j, t: (0, j, 0, 0))
    return pl.pallas_call(
        finish_kernel,
        grid_spec=pltpu.PrefetchScalarGridSpec(
            num_scalar_prefetch=1,
            grid=(NZ,),
            in_specs=[pl.BlockSpec((tokens, cols), lambda j, t: (0, 0)), spec_a, spec_a],
            out_specs=pl.BlockSpec((cols, n_blk), lambda j, t: (0, j)),
            scratch_shapes=[pltpu.VMEM((tokens, cols), BF16), pltpu.VMEM((EXAMPLES, cols, T_EX), BF16)],
        ),
        out_shape=jax.ShapeDtypeStruct((cols, NZ * n_blk), F32),
        compiler_params=pltpu.CompilerParams(vmem_limit_bytes=24 * 2**20),
        cost_estimate=pl.CostEstimate(
            flops=2 * tokens * cols * NZ * n_blk, bytes_accessed=4 * cols * NZ * n_blk + 4 * tokens * n_blk * NZ, transcendentals=0
        ),
    )(table, g_all, own, other)


def places(y, z, c, x):
    steps = jnp.array(Y_STEPS, jnp.int32)

    def place(block, core):
        return (((y + steps[block // NZ]) % NY) * NZ + (z - block % NZ) % NZ) * NC + core

    near = jnp.arange(3 * NZ, dtype=jnp.int32)
    near = jnp.concatenate([place(near, c), place(near, 1 - c)]).reshape(NX, -1)
    far = 3 * NZ + jnp.arange(NZ, dtype=jnp.int32)
    y_all = jnp.arange(NY, dtype=jnp.int32) * NC
    slots = (x - jnp.arange(NX, dtype=jnp.int32)) % NX
    return jnp.concatenate([near[slots].reshape(-1), place(far, c), place(far, 1 - c), y_all + c, y_all + 1 - c]).astype(jnp.int32)


def rotate_acts(acts, act_basis):
    gathered = lax.all_gather(acts, "z", axis=1, tiled=True)
    basis = lax.all_to_all(act_basis, "z", 1, 0, tiled=True)
    partial = jnp.dot(gathered, basis, preferred_element_type=F32)
    terms = lax.all_to_all(partial, ("y", "core"), 0, 0, tiled=True)
    piece = terms.reshape(NY * NC, T_EX, -1).sum(0).astype(BF16)
    own = lax.all_gather(piece, ("y", "z"), axis=0).reshape(NY, NZ, T_EX, -1)
    return own, shift(own, "core", 1)


def rotate_grads(grads, grad_basis, x):
    basis = grad_basis.T
    basis_other = shift(basis, "core", 1)
    load = jnp.concatenate(ring_z(grads), axis=0)
    h = load.shape[0] // 2
    below, above = shift(load, "y", 1), shift(load, "y", -1)
    far = jnp.concatenate([shift(below[:h], "y", 1), shift(above[h:], "y", -1)], axis=0)

    mine, theirs = product(jnp.concatenate([load, below, above], axis=0), basis, basis_other)
    partial = jnp.concatenate([mine, shift(theirs, "core", 1)], axis=0)
    partial = partial.reshape(NX, -1, partial.shape[1])
    total = lax.dynamic_index_in_dim(partial, x, 0, False)
    for d in (1, 2, -1):
        total = total + shift(lax.dynamic_index_in_dim(partial, (x + d) % NX, 0, False), "x", d)
    total = total.astype(BF16)
    out = [total, shift(total, "x", 1), shift(total, "x", 2), shift(total, "x", -1)]

    mine, theirs = product(far, basis, basis_other)
    partial = jnp.concatenate([mine, shift(theirs, "core", 1)], axis=0)
    out.append(lax.psum(partial, "x").astype(BF16))
    return jnp.concatenate(out, axis=0)


def body(acts, grads, act_basis, grad_basis):
    y, z, c, x = (lax.axis_index(a) for a in ("y", "z", "core", "x"))
    own, other = rotate_acts(acts, act_basis)
    g_all = rotate_grads(grads, grad_basis, x)
    return finish(places(y, z, c, x), g_all, own, other)


def solution(mesh):
    wide = ("y", "z", "core")
    return jax.shard_map(
        body,
        mesh=Mesh(mesh.devices.reshape(NY, NZ, NC, NX), wide + ("x",)),
        in_specs=(P(None, wide), P(wide, "x"), P(wide, "x"), P("x", wide)),
        out_specs=P(wide, "x"),
        check_vma=False,
    )
```

```python
import jax
import jax.numpy as jnp
from jax import lax
from jax.experimental import pallas as pl
from jax.experimental.pallas import tpu as pltpu
from jax.sharding import Mesh, PartitionSpec as P

EXAMPLES = 8
T_EX = 128
NY, NZ, NC, NX = 4, 8, 2, 4
ROWS = 16
STEPS = 4
BF16, F32 = jnp.bfloat16, jnp.float32
SIZES = {"y": NY, "z": NZ, "core": NC, "x": NX}


def shift(v, axis, d):
    n = SIZES[axis]
    return lax.ppermute(v, axis, [(i, (i + d) % n) for i in range(n)])


def ring_z(v):
    up, down = [v], [v]
    for _ in range(4):
        up.append(shift(up[-1], "z", 1))
    for _ in range(3):
        down.append(shift(down[-1], "z", -1))
    return up + down[:0:-1]


def product_kernel(at_ref, *refs):
    parts, (b_ref, b_other_ref, o_ref) = refs[:-3], refs[-3:]
    k, c = pl.program_id(0), at_ref[2]

    @pl.when(k == 0)
    def _():
        o_ref[...] = jnp.zeros_like(o_ref)

    row = 0
    for x_ref in parts:
        n = x_ref.shape[0]
        for b, h in ((b_ref, c), (b_other_ref, 1 - c)):
            o_ref[h, row : row + n, :] += lax.dot_general(
                x_ref[...], b[...], (((1,), (1,)), ((), ())), preferred_element_type=F32
            )
        row += n


def product(at, parts, b, b_other):
    rows, depth = sum(p.shape[0] for p in parts), parts[0].shape[1]
    cols, step = b.shape[0], depth // STEPS
    spec_b = pl.BlockSpec((cols, step), lambda k, t: (0, k))
    return pl.pallas_call(
        product_kernel,
        grid_spec=pltpu.PrefetchScalarGridSpec(
            num_scalar_prefetch=1,
            grid=(STEPS,),
            in_specs=[pl.BlockSpec((p.shape[0], step), lambda k, t: (0, k)) for p in parts] + [spec_b, spec_b],
            out_specs=pl.BlockSpec((NC, rows, cols), lambda k, t: (0, 0, 0)),
        ),
        out_shape=jax.ShapeDtypeStruct((NC, rows, cols), F32),
        compiler_params=pltpu.CompilerParams(vmem_limit_bytes=24 * 2**20),
        cost_estimate=pl.CostEstimate(
            flops=4 * rows * cols * depth, bytes_accessed=2 * depth * (rows + 2 * cols) + 8 * rows * cols, transcendentals=0
        ),
    )(at, *parts, b, b_other)


def sum_over_x(partial):
    cols = partial.shape[2]
    terms = lax.all_to_all(partial.reshape(-1, cols), ("core", "x"), 0, 0, tiled=True)
    total = terms.reshape(NC, NX, -1, cols).sum(1).astype(BF16)
    return total.reshape(-1, cols)


def finish_kernel(at_ref, near_ref, far_ref, own_ref, other_ref, o_ref, rows, turned):
    y, z, c = at_ref[0], at_ref[1], at_ref[2]

    @pl.when(pl.program_id(0) == 0)
    def _():
        chunks = ((near_ref, 0, (0,)), (near_ref, NZ * NC // NX, (-1, 1)), (far_ref, 0, (2,)))
        for ref, skip, y_steps in chunks:
            each = len(y_steps) * NZ // NX
            stride = ref.shape[0] // (NX * ROWS)
            for j in range(NX * NC * each):
                slot, s = j // (NC * each), (j // each) % NC
                i = slot * stride + skip + s * each + j % each
                block = slot * each + j % each
                y_at = lax.rem(y + (y_steps[block // NZ] + NY), NY)
                z_at = lax.rem(z + (NZ - block % NZ), NZ)
                to = pl.multiple_of(((y_at * NZ + z_at) * NC + s) * ROWS, ROWS)
                rows[pl.ds(to, ROWS), :] = ref[i * ROWS : (i + 1) * ROWS, :]
        for e in range(EXAMPLES):
            turned[e] = rows[e * T_EX : (e + 1) * T_EX, :].T

    for i in range(EXAMPLES):
        ref, core = (own_ref, c) if i < NY else (other_ref, 1 - c)
        r = jnp.dot(turned[(i % NY) * NC + core], ref[0, i % NY], preferred_element_type=F32)
        r = r * r
        if i > 0:
            r = r + o_ref[...]
        if i == EXAMPLES - 1:
            r = r * (1.0 / (EXAMPLES * T_EX))
        o_ref[...] = r


def finish(at, g_parts, own, other):
    tokens, cols = sum(g.shape[0] for g in g_parts), g_parts[0].shape[1]
    n_blk = own.shape[3]
    spec_a = pl.BlockSpec((1, NY, T_EX, n_blk), lambda j, t: (j, 0, 0, 0))
    return pl.pallas_call(
        finish_kernel,
        grid_spec=pltpu.PrefetchScalarGridSpec(
            num_scalar_prefetch=1,
            grid=(NZ,),
            in_specs=[pl.BlockSpec(g.shape, lambda j, t: (0, 0)) for g in g_parts] + [spec_a, spec_a],
            out_specs=pl.BlockSpec((cols, n_blk), lambda j, t: (0, j)),
            scratch_shapes=[pltpu.VMEM((tokens, cols), BF16), pltpu.VMEM((EXAMPLES, cols, T_EX), BF16)],
        ),
        out_shape=jax.ShapeDtypeStruct((cols, NZ * n_blk), F32),
        compiler_params=pltpu.CompilerParams(vmem_limit_bytes=24 * 2**20),
        cost_estimate=pl.CostEstimate(
            flops=2 * tokens * cols * NZ * n_blk, bytes_accessed=4 * cols * NZ * n_blk + 4 * tokens * n_blk * NZ, transcendentals=0
        ),
    )(at, *g_parts, own, other)


def exchange_acts(acts, act_basis, x):
    depth, n_blk = act_basis.shape[0], act_basis.shape[1] // NZ
    quarter = acts.shape[0] // NX
    halves = n_blk // depth
    mine = lax.dynamic_slice_in_dim(acts, x * quarter, quarter, 0)
    basis = act_basis.reshape(depth, NZ, halves, depth).transpose(1, 2, 0, 3).reshape(NZ, n_blk, depth)
    sent = jnp.concatenate([basis, jnp.broadcast_to(mine[None], (NZ, quarter, depth))], axis=1)
    got = lax.all_to_all(sent, "z", 0, 0, tiled=True)
    basis = got[:, :n_blk].reshape(NZ, halves, depth, depth).transpose(0, 2, 1, 3).reshape(NZ * depth, n_blk)
    rows = got[:, n_blk:].transpose(1, 0, 2).reshape(quarter, NZ * depth)
    return lax.all_gather(rows, "x", axis=0, tiled=True), basis


def after(values, *others):
    return lax.optimization_barrier((tuple(values), others))[0]


def body(acts, grads, act_basis, grad_basis):
    y, z, c, x = (lax.axis_index(a) for a in ("y", "z", "core", "x"))
    at = jnp.stack([y, z, c]).astype(jnp.int32)
    basis = grad_basis.T
    basis_other = shift(basis, "core", 1)
    rows, basis_acts = exchange_acts(acts, act_basis, x)
    load = jnp.concatenate(ring_z(grads), axis=0)
    h = load.shape[0] // 2

    below, above = shift(load, "y", 1), shift(load, "y", -1)
    product_load = product(at, [load], basis, basis_other)
    (rows,) = after([rows], load, product_load)
    partial = jnp.dot(rows, basis_acts, preferred_element_type=F32)
    terms = lax.all_to_all(partial, ("y", "core"), 0, 0, tiled=True)
    piece = terms.reshape(NY * NC, T_EX, -1).sum(0).astype(BF16)

    far = [shift(below[:h], "y", 1), shift(above[h:], "y", -1)]
    product_near = product(at, [below, above], basis, basis_other)
    along_y = lax.all_to_all(jnp.broadcast_to(piece[None], (NY,) + piece.shape), "y", 0, 0, tiled=True)
    (along_y,) = after([along_y], below, above)
    own = lax.all_gather(along_y, "z", axis=0)
    total_load = sum_over_x(product_load)

    far = after(far, product_near, along_y, total_load)
    product_far = product(at, far, basis, basis_other)
    total_far = sum_over_x(product_far)
    total_near = sum_over_x(product_near)
    g_load = lax.all_gather(jnp.concatenate([total_load, total_near], axis=0), "x", axis=0, tiled=True)
    (total_far,) = after([total_far], g_load)
    g_far = lax.all_gather(total_far, "x", axis=0, tiled=True)
    (own,) = after([own], g_far)
    return finish(at, [g_load, g_far], own, shift(own, "core", 1))


def solution(mesh):
    wide = ("y", "z", "core")
    return jax.shard_map(
        body,
        mesh=Mesh(mesh.devices.reshape(NY, NZ, NC, NX), wide + ("x",)),
        in_specs=(P(None, wide), P(wide, "x"), P(wide, "x"), P("x", wide)),
        out_specs=P(wide, "x"),
        check_vma=False,
    )
```

```python
import jax
import jax.numpy as jnp
from jax import lax
from jax.experimental import pallas as pl
from jax.experimental.pallas import tpu as pltpu
from jax.sharding import Mesh, PartitionSpec as P

EXAMPLES = 8
T_EX = 128
NY, NZ, NC, NX = 4, 8, 2, 4
ROWS = 16
STEPS = 4
BF16, F32 = jnp.bfloat16, jnp.float32
SIZES = {"y": NY, "z": NZ, "core": NC, "x": NX}


def shift(v, axis, d):
    n = SIZES[axis]
    return lax.ppermute(v, axis, [(i, (i + d) % n) for i in range(n)])


def ring_z(v):
    up, down = [v], [v]
    for _ in range(4):
        up.append(shift(up[-1], "z", 1))
    for _ in range(3):
        down.append(shift(down[-1], "z", -1))
    return up + down[:0:-1]


def product_kernel(at_ref, *refs):
    parts, (b_ref, b_other_ref, o_ref) = refs[:-3], refs[-3:]
    k, c = pl.program_id(0), at_ref[2]

    @pl.when(k == 0)
    def _():
        o_ref[...] = jnp.zeros_like(o_ref)

    x = jnp.concatenate([p[...] for p in parts], axis=0) if len(parts) > 1 else parts[0][...]
    for b, h in ((b_ref, c), (b_other_ref, 1 - c)):
        o_ref[h] += lax.dot_general(x, b[...], (((1,), (1,)), ((), ())), preferred_element_type=F32)


def product(at, parts, b, b_other):
    rows, depth = sum(p.shape[0] for p in parts), parts[0].shape[1]
    cols, step = b.shape[0], depth // STEPS
    spec_b = pl.BlockSpec((cols, step), lambda k, t: (0, k))
    return pl.pallas_call(
        product_kernel,
        grid_spec=pltpu.PrefetchScalarGridSpec(
            num_scalar_prefetch=1,
            grid=(STEPS,),
            in_specs=[pl.BlockSpec((p.shape[0], step), lambda k, t: (0, k)) for p in parts] + [spec_b, spec_b],
            out_specs=pl.BlockSpec((NC, rows, cols), lambda k, t: (0, 0, 0)),
        ),
        out_shape=jax.ShapeDtypeStruct((NC, rows, cols), F32),
        compiler_params=pltpu.CompilerParams(vmem_limit_bytes=54 * 2**20),
        cost_estimate=pl.CostEstimate(
            flops=4 * rows * cols * depth, bytes_accessed=2 * depth * (rows + 2 * cols) + 8 * rows * cols, transcendentals=0
        ),
    )(at, *parts, b, b_other)


def sum_over_x(partial):
    cols = partial.shape[2]
    terms = lax.all_to_all(partial.reshape(-1, cols), ("core", "x"), 0, 0, tiled=True)
    total = terms.reshape(NC, NX, -1, cols).sum(1).astype(BF16)
    return total.reshape(-1, cols)


def finish_kernel(at_ref, near_ref, far_ref, own_ref, other_ref, o_ref, rows, turned):
    y, z, c = at_ref[0], at_ref[1], at_ref[2]

    @pl.when(pl.program_id(0) == 0)
    def _():
        chunks = ((near_ref, 0, (0,)), (near_ref, NZ * NC // NX, (-1, 1)), (far_ref, 0, (2,)))
        for ref, skip, y_steps in chunks:
            each = len(y_steps) * NZ // NX
            stride = ref.shape[0] // (NX * ROWS)
            for j in range(NX * NC * each):
                slot, s = j // (NC * each), (j // each) % NC
                i = slot * stride + skip + s * each + j % each
                block = slot * each + j % each
                y_at = lax.rem(y + (y_steps[block // NZ] + NY), NY)
                z_at = lax.rem(z + (NZ - block % NZ), NZ)
                to = pl.multiple_of(((y_at * NZ + z_at) * NC + s) * ROWS, ROWS)
                rows[pl.ds(to, ROWS), :] = ref[i * ROWS : (i + 1) * ROWS, :]
        for e in range(EXAMPLES):
            turned[e] = rows[e * T_EX : (e + 1) * T_EX, :].T

    for i in range(EXAMPLES):
        ref, core = (own_ref, c) if i < NY else (other_ref, 1 - c)
        r = jnp.dot(turned[(i % NY) * NC + core], ref[0, i % NY], preferred_element_type=F32)
        r = r * r
        if i > 0:
            r = r + o_ref[...]
        if i == EXAMPLES - 1:
            r = r * (1.0 / (EXAMPLES * T_EX))
        o_ref[...] = r


def finish(at, g_parts, own, other):
    tokens, cols = sum(g.shape[0] for g in g_parts), g_parts[0].shape[1]
    n_blk = own.shape[3]
    spec_a = pl.BlockSpec((1, NY, T_EX, n_blk), lambda j, t: (j, 0, 0, 0))
    return pl.pallas_call(
        finish_kernel,
        grid_spec=pltpu.PrefetchScalarGridSpec(
            num_scalar_prefetch=1,
            grid=(NZ,),
            in_specs=[pl.BlockSpec(g.shape, lambda j, t: (0, 0)) for g in g_parts] + [spec_a, spec_a],
            out_specs=pl.BlockSpec((cols, n_blk), lambda j, t: (0, j)),
            scratch_shapes=[pltpu.VMEM((tokens, cols), BF16), pltpu.VMEM((EXAMPLES, cols, T_EX), BF16)],
        ),
        out_shape=jax.ShapeDtypeStruct((cols, NZ * n_blk), F32),
        compiler_params=pltpu.CompilerParams(vmem_limit_bytes=24 * 2**20),
        cost_estimate=pl.CostEstimate(
            flops=2 * tokens * cols * NZ * n_blk, bytes_accessed=4 * cols * NZ * n_blk + 4 * tokens * n_blk * NZ, transcendentals=0
        ),
    )(at, *g_parts, own, other)


def gather_x(v):
    copies = jnp.broadcast_to(v[None], (NX,) + v.shape)
    return lax.all_to_all(copies, "x", 0, 0, tiled=True).reshape((-1,) + v.shape[1:])


def after(values, *others):
    return lax.optimization_barrier((tuple(values), others))[0]


def body(acts, grads, act_basis, grad_basis):
    y, z, c = (lax.axis_index(a) for a in ("y", "z", "core"))
    at = jnp.stack([y, z, c]).astype(jnp.int32)
    basis = grad_basis.T
    basis_other = shift(basis, "core", 1)
    rows = lax.all_gather(acts, "z", axis=1, tiled=True)
    load = jnp.concatenate(ring_z(grads), axis=0)
    (act_basis,) = after([act_basis], load)
    basis_acts = lax.all_to_all(act_basis, "z", 1, 0, tiled=True)
    h = load.shape[0] // 2

    below, above = shift(load, "y", 1), shift(load, "y", -1)
    product_load = product(at, [load], basis, basis_other)
    (rows,) = after([rows], load, product_load)
    partial = jnp.dot(rows, basis_acts, preferred_element_type=F32)
    terms = lax.all_to_all(partial, ("y", "core"), 0, 0, tiled=True)
    piece = terms.reshape(NY * NC, T_EX, -1).sum(0).astype(BF16)

    far = [shift(below[:h], "y", 1), shift(above[h:], "y", -1)]
    product_near = product(at, [below, above], basis, basis_other)
    along_y = lax.all_to_all(jnp.broadcast_to(piece[None], (NY,) + piece.shape), "y", 0, 0, tiled=True)
    (along_y,) = after([along_y], below, above)
    own = lax.all_gather(along_y, "z", axis=0)
    total_load = sum_over_x(product_load)

    far = after(far, product_near, along_y, total_load)
    product_far = product(at, far, basis, basis_other)
    total_far = sum_over_x(product_far)
    total_near = sum_over_x(product_near)
    g_load = lax.all_gather(jnp.concatenate([total_load, total_near], axis=0), "x", axis=0, tiled=True)
    (total_far,) = after([total_far], g_load)
    (own,) = after([own], total_far)
    g_far = gather_x(total_far)
    return finish(at, [g_load, g_far], own, shift(own, "core", 1))


def solution(mesh):
    wide = ("y", "z", "core")
    return jax.shard_map(
        body,
        mesh=Mesh(mesh.devices.reshape(NY, NZ, NC, NX), wide + ("x",)),
        in_specs=(P(None, wide), P(wide, "x"), P(wide, "x"), P("x", wide)),
        out_specs=P(wide, "x"),
        check_vma=False,
    )
```

```python
import jax
import jax.numpy as jnp
from jax import lax
from jax.experimental import pallas as pl
from jax.experimental.pallas import tpu as pltpu
from jax.sharding import Mesh, PartitionSpec as P

EXAMPLES = 8
T_EX = 128
NY, NZ, NC, NX = 4, 8, 2, 4
ROWS = 16
STEPS = 4
BF16, F32 = jnp.bfloat16, jnp.float32
SIZES = {"y": NY, "z": NZ, "core": NC, "x": NX}


def shift(v, axis, d):
    n = SIZES[axis]
    return lax.ppermute(v, axis, [(i, (i + d) % n) for i in range(n)])


def ring_z(v):
    up, down = [v], [v]
    for _ in range(4):
        up.append(shift(up[-1], "z", 1))
    for _ in range(3):
        down.append(shift(down[-1], "z", -1))
    return up + down[:0:-1]


def product_kernel(at_ref, *refs):
    parts, (b_ref, b_other_ref, o_ref) = refs[:-3], refs[-3:]
    k, c = pl.program_id(0), at_ref[2]

    @pl.when(k == 0)
    def _():
        o_ref[...] = jnp.zeros_like(o_ref)

    x = jnp.concatenate([p[...] for p in parts], axis=0) if len(parts) > 1 else parts[0][...]
    for b, h in ((b_ref, c), (b_other_ref, 1 - c)):
        o_ref[h] += lax.dot_general(x, b[...], (((1,), (1,)), ((), ())), preferred_element_type=F32)


def product(at, parts, b, b_other):
    rows, depth = sum(p.shape[0] for p in parts), parts[0].shape[1]
    cols, step = b.shape[0], depth // STEPS
    spec_b = pl.BlockSpec((cols, step), lambda k, t: (0, k))
    return pl.pallas_call(
        product_kernel,
        grid_spec=pltpu.PrefetchScalarGridSpec(
            num_scalar_prefetch=1,
            grid=(STEPS,),
            in_specs=[pl.BlockSpec((p.shape[0], step), lambda k, t: (0, k)) for p in parts] + [spec_b, spec_b],
            out_specs=pl.BlockSpec((NC, rows, cols), lambda k, t: (0, 0, 0)),
        ),
        out_shape=jax.ShapeDtypeStruct((NC, rows, cols), F32),
        compiler_params=pltpu.CompilerParams(vmem_limit_bytes=54 * 2**20),
        cost_estimate=pl.CostEstimate(
            flops=4 * rows * cols * depth, bytes_accessed=2 * depth * (rows + 2 * cols) + 8 * rows * cols, transcendentals=0
        ),
    )(at, *parts, b, b_other)


def sum_over_x(partial):
    cols = partial.shape[2]
    terms = lax.all_to_all(partial.reshape(-1, cols), ("core", "x"), 0, 0, tiled=True)
    total = terms.reshape(NC, NX, -1, cols).sum(1).astype(BF16)
    return total.reshape(-1, cols)


def finish_kernel(at_ref, near_ref, far_ref, own_ref, other_ref, o_ref, rows, turned):
    y, z, c = at_ref[0], at_ref[1], at_ref[2]

    @pl.when(pl.program_id(0) == 0)
    def _():
        chunks = ((near_ref, 0, (0,)), (near_ref, NZ * NC // NX, (-1, 1)), (far_ref, 0, (2,)))
        for ref, skip, y_steps in chunks:
            each = len(y_steps) * NZ // NX
            stride = ref.shape[0] // (NX * ROWS)
            for j in range(NX * NC * each):
                slot, s = j // (NC * each), (j // each) % NC
                i = slot * stride + skip + s * each + j % each
                block = slot * each + j % each
                y_at = lax.rem(y + (y_steps[block // NZ] + NY), NY)
                z_at = lax.rem(z + (NZ - block % NZ), NZ)
                to = pl.multiple_of(((y_at * NZ + z_at) * NC + s) * ROWS, ROWS)
                rows[pl.ds(to, ROWS), :] = ref[i * ROWS : (i + 1) * ROWS, :]
        for e in range(EXAMPLES):
            turned[e] = rows[e * T_EX : (e + 1) * T_EX, :].T

    for i in range(EXAMPLES):
        ref, core = (own_ref, c) if i < NY else (other_ref, 1 - c)
        r = jnp.dot(turned[(i % NY) * NC + core], ref[0, i % NY], preferred_element_type=F32)
        r = r * r
        if i > 0:
            r = r + o_ref[...]
        if i == EXAMPLES - 1:
            r = r * (1.0 / (EXAMPLES * T_EX))
        o_ref[...] = r


def finish(at, g_parts, own, other):
    tokens, cols = sum(g.shape[0] for g in g_parts), g_parts[0].shape[1]
    n_blk = own.shape[3]
    spec_a = pl.BlockSpec((1, NY, T_EX, n_blk), lambda j, t: (j, 0, 0, 0))
    return pl.pallas_call(
        finish_kernel,
        grid_spec=pltpu.PrefetchScalarGridSpec(
            num_scalar_prefetch=1,
            grid=(NZ,),
            in_specs=[pl.BlockSpec(g.shape, lambda j, t: (0, 0)) for g in g_parts] + [spec_a, spec_a],
            out_specs=pl.BlockSpec((cols, n_blk), lambda j, t: (0, j)),
            scratch_shapes=[pltpu.VMEM((tokens, cols), BF16), pltpu.VMEM((EXAMPLES, cols, T_EX), BF16)],
        ),
        out_shape=jax.ShapeDtypeStruct((cols, NZ * n_blk), F32),
        compiler_params=pltpu.CompilerParams(vmem_limit_bytes=54 * 2**20),
        cost_estimate=pl.CostEstimate(
            flops=2 * tokens * cols * NZ * n_blk, bytes_accessed=4 * cols * NZ * n_blk + 4 * tokens * n_blk * NZ, transcendentals=0
        ),
    )(at, *g_parts, own, other)


def gather_x(v):
    copies = jnp.broadcast_to(v[None], (NX,) + v.shape)
    return lax.all_to_all(copies, "x", 0, 0, tiled=True).reshape((-1,) + v.shape[1:])


def after(values, *others):
    return lax.optimization_barrier((tuple(values), others))[0]


def body(acts, grads, act_basis, grad_basis):
    y, z, c = (lax.axis_index(a) for a in ("y", "z", "core"))
    at = jnp.stack([y, z, c]).astype(jnp.int32)
    basis = grad_basis.T
    basis_other = shift(basis, "core", 1)
    rows = lax.all_gather(acts, "z", axis=1, tiled=True)
    load = jnp.concatenate(ring_z(grads), axis=0)
    h = load.shape[0] // 2

    below, above = shift(load, "y", 1), shift(load, "y", -1)
    product_load = product(at, [load], basis, basis_other)
    (act_basis,) = after([act_basis], product_load)
    basis_acts = lax.all_to_all(act_basis, "z", 1, 0, tiled=True)
    (rows,) = after([rows], load, product_load)
    partial = jnp.dot(rows, basis_acts, preferred_element_type=F32)
    terms = lax.all_to_all(partial, ("y", "core"), 0, 0, tiled=True)
    piece = terms.reshape(NY * NC, T_EX, -1).sum(0).astype(BF16)

    far = [shift(below[:h], "y", 1), shift(above[h:], "y", -1)]
    product_near = product(at, [below, above], basis, basis_other)
    along_y = lax.all_to_all(jnp.broadcast_to(piece[None], (NY,) + piece.shape), "y", 0, 0, tiled=True)
    (along_y,) = after([along_y], product_near, *far)
    own = lax.all_gather(along_y, "z", axis=0)
    total_load = sum_over_x(product_load)

    far = after(far, product_near, along_y, total_load)
    product_far = product(at, far, basis, basis_other)
    total_far = sum_over_x(product_far)
    total_near = sum_over_x(product_near)
    g_load = lax.all_gather(jnp.concatenate([total_load, total_near], axis=0), "x", axis=0, tiled=True)
    (total_far,) = after([total_far], g_load)
    (own,) = after([own], total_far)
    g_far = gather_x(total_far)
    return finish(at, [g_load, g_far], own, shift(own, "core", 1))


def solution(mesh):
    wide = ("y", "z", "core")
    return jax.shard_map(
        body,
        mesh=Mesh(mesh.devices.reshape(NY, NZ, NC, NX), wide + ("x",)),
        in_specs=(P(None, wide), P(wide, "x"), P(wide, "x"), P("x", wide)),
        out_specs=P(wide, "x"),
        check_vma=False,
    )
```

```python
import jax
import jax.numpy as jnp
from jax import lax
from jax.experimental import pallas as pl
from jax.experimental.pallas import tpu as pltpu
from jax.sharding import Mesh, PartitionSpec as P

EXAMPLES = 8
T_EX = 128
NY, NZ, NC, NX = 4, 8, 2, 4
ROWS = 16
STEPS = 4
BF16, F32 = jnp.bfloat16, jnp.float32
SIZES = {"y": NY, "z": NZ, "core": NC, "x": NX}


def shift(v, axis, d):
    n = SIZES[axis]
    return lax.ppermute(v, axis, [(i, (i + d) % n) for i in range(n)])


def ring_z(v):
    up, down = [v], [v]
    for _ in range(4):
        up.append(shift(up[-1], "z", 1))
    for _ in range(3):
        down.append(shift(down[-1], "z", -1))
    return up + down[:0:-1]


def product_kernel(at_ref, *refs):
    parts, (b_ref, b_other_ref, o_ref) = refs[:-3], refs[-3:]
    k, c = pl.program_id(0), at_ref[2]

    @pl.when(k == 0)
    def _():
        o_ref[...] = jnp.zeros_like(o_ref)

    x = jnp.concatenate([p[...] for p in parts], axis=0) if len(parts) > 1 else parts[0][...]
    for b, h in ((b_ref, c), (b_other_ref, 1 - c)):
        o_ref[h] += lax.dot_general(x, b[...], (((1,), (1,)), ((), ())), preferred_element_type=F32)


def product(at, parts, b, b_other):
    rows, depth = sum(p.shape[0] for p in parts), parts[0].shape[1]
    cols, step = b.shape[0], depth // STEPS
    spec_b = pl.BlockSpec((cols, step), lambda k, t: (0, k))
    return pl.pallas_call(
        product_kernel,
        grid_spec=pltpu.PrefetchScalarGridSpec(
            num_scalar_prefetch=1,
            grid=(STEPS,),
            in_specs=[pl.BlockSpec((p.shape[0], step), lambda k, t: (0, k)) for p in parts] + [spec_b, spec_b],
            out_specs=pl.BlockSpec((NC, rows, cols), lambda k, t: (0, 0, 0)),
        ),
        out_shape=jax.ShapeDtypeStruct((NC, rows, cols), F32),
        compiler_params=pltpu.CompilerParams(vmem_limit_bytes=54 * 2**20),
        cost_estimate=pl.CostEstimate(
            flops=4 * rows * cols * depth, bytes_accessed=2 * depth * (rows + 2 * cols) + 8 * rows * cols, transcendentals=0
        ),
    )(at, *parts, b, b_other)


def sum_over_x(partial):
    cols = partial.shape[2]
    terms = lax.all_to_all(partial.reshape(-1, cols), ("core", "x"), 0, 0, tiled=True)
    total = terms.reshape(NC, NX, -1, cols).sum(1).astype(BF16)
    return total.reshape(-1, cols)


def finish_kernel(at_ref, g_ref, own_ref, other_ref, o_ref, rows, turned):
    y, z, c = at_ref[0], at_ref[1], at_ref[2]

    @pl.when(pl.program_id(0) == 0)
    def _():
        stride = g_ref.shape[0] // (NX * ROWS)
        one = NZ // NX
        for skip, y_steps in ((0, (0,)), (one, (-1, 1)), (3 * one, (2,))):
            each = len(y_steps) * one
            for j in range(NX * NC * each):
                slot, s = j // (NC * each), (j // each) % NC
                i = slot * stride + s * NY * one + skip + j % each
                block = slot * each + j % each
                y_at = lax.rem(y + (y_steps[block // NZ] + NY), NY)
                z_at = lax.rem(z + (NZ - block % NZ), NZ)
                to = pl.multiple_of(((y_at * NZ + z_at) * NC + s) * ROWS, ROWS)
                rows[pl.ds(to, ROWS), :] = g_ref[i * ROWS : (i + 1) * ROWS, :]
        for e in range(EXAMPLES):
            turned[e] = rows[e * T_EX : (e + 1) * T_EX, :].T

    for i in range(EXAMPLES):
        ref, core = (own_ref, c) if i < NY else (other_ref, 1 - c)
        r = jnp.dot(turned[(i % NY) * NC + core], ref[0, i % NY], preferred_element_type=F32)
        r = r * r
        if i > 0:
            r = r + o_ref[...]
        if i == EXAMPLES - 1:
            r = r * (1.0 / (EXAMPLES * T_EX))
        o_ref[...] = r


def finish(at, g_all, own, other):
    tokens, cols = g_all.shape
    n_blk = own.shape[3]
    spec_a = pl.BlockSpec((1, NY, T_EX, n_blk), lambda j, t: (j, 0, 0, 0))
    return pl.pallas_call(
        finish_kernel,
        grid_spec=pltpu.PrefetchScalarGridSpec(
            num_scalar_prefetch=1,
            grid=(NZ,),
            in_specs=[pl.BlockSpec((tokens, cols), lambda j, t: (0, 0)), spec_a, spec_a],
            out_specs=pl.BlockSpec((cols, n_blk), lambda j, t: (0, j)),
            scratch_shapes=[pltpu.VMEM((tokens, cols), BF16), pltpu.VMEM((EXAMPLES, cols, T_EX), BF16)],
        ),
        out_shape=jax.ShapeDtypeStruct((cols, NZ * n_blk), F32),
        compiler_params=pltpu.CompilerParams(vmem_limit_bytes=24 * 2**20),
        cost_estimate=pl.CostEstimate(
            flops=2 * tokens * cols * NZ * n_blk, bytes_accessed=4 * cols * NZ * n_blk + 4 * tokens * n_blk * NZ, transcendentals=0
        ),
    )(at, g_all, own, other)


def after(values, *others):
    return lax.optimization_barrier((tuple(values), others))[0]


def body(acts, grads, act_basis, grad_basis):
    y, z, c = (lax.axis_index(a) for a in ("y", "z", "core"))
    at = jnp.stack([y, z, c]).astype(jnp.int32)
    basis = grad_basis.T
    basis_other = shift(basis, "core", 1)
    rows = lax.all_gather(acts, "z", axis=1, tiled=True)
    load = jnp.concatenate(ring_z(grads), axis=0)
    h = load.shape[0] // 2

    below, above = shift(load, "y", 1), shift(load, "y", -1)
    product_load = product(at, [load], basis, basis_other)
    (act_basis,) = after([act_basis], product_load)
    basis_acts = lax.all_to_all(act_basis, "z", 1, 0, tiled=True)
    (rows,) = after([rows], load, product_load)
    partial = jnp.dot(rows, basis_acts, preferred_element_type=F32)
    terms = lax.all_to_all(partial, ("y", "core"), 0, 0, tiled=True)
    piece = terms.reshape(NY * NC, T_EX, -1).sum(0).astype(BF16)

    far = [shift(below[:h], "y", 1), shift(above[h:], "y", -1)]
    product_near = product(at, [below, above], basis, basis_other)
    along_y = lax.all_to_all(jnp.broadcast_to(piece[None], (NY,) + piece.shape), "y", 0, 0, tiled=True)
    (along_y,) = after([along_y], product_near, *far)
    own = lax.all_gather(along_y, "z", axis=0)

    cols = product_near.shape[2]
    far = after(far, product_near, along_y)
    chunks = (product_load, product_near, product(at, far, basis, basis_other))
    total = sum_over_x(jnp.concatenate([p.reshape(NC * NX, -1, cols) for p in chunks], axis=1))
    (own,) = after([own], total)
    g_all = lax.all_gather(total, "x", axis=0, tiled=True)
    return finish(at, g_all, own, shift(own, "core", 1))


def solution(mesh):
    wide = ("y", "z", "core")
    return jax.shard_map(
        body,
        mesh=Mesh(mesh.devices.reshape(NY, NZ, NC, NX), wide + ("x",)),
        in_specs=(P(None, wide), P(wide, "x"), P(wide, "x"), P("x", wide)),
        out_specs=P(wide, "x"),
        check_vma=False,
    )
```

```python
import jax
import jax.numpy as jnp
from jax import lax
from jax.experimental import pallas as pl
from jax.experimental.pallas import tpu as pltpu
from jax.sharding import Mesh, PartitionSpec as P

EXAMPLES = 8
T_EX = 128
NY, NZ, NC, NX = 4, 8, 2, 4
ROWS = 16
STEPS = 4
BF16, F32 = jnp.bfloat16, jnp.float32
SIZES = {"y": NY, "z": NZ, "core": NC, "x": NX}


def shift(v, axis, d):
    n = SIZES[axis]
    return lax.ppermute(v, axis, [(i, (i + d) % n) for i in range(n)])


def ring_z(v):
    up, down = [v], [v]
    for _ in range(4):
        up.append(shift(up[-1], "z", 1))
    for _ in range(3):
        down.append(shift(down[-1], "z", -1))
    return up + down[:0:-1]


def product_kernel(at_ref, *refs):
    parts, (b_ref, b_other_ref, o_ref) = refs[:-3], refs[-3:]
    k, c = pl.program_id(0), at_ref[2]

    @pl.when(k == 0)
    def _():
        o_ref[...] = jnp.zeros_like(o_ref)

    x = jnp.concatenate([p[...] for p in parts], axis=0) if len(parts) > 1 else parts[0][...]
    for b, h in ((b_ref, c), (b_other_ref, 1 - c)):
        o_ref[h] += lax.dot_general(x, b[...], (((1,), (1,)), ((), ())), preferred_element_type=F32)


def product(at, parts, b, b_other):
    rows, depth = sum(p.shape[0] for p in parts), parts[0].shape[1]
    cols, step = b.shape[0], depth // STEPS
    spec_b = pl.BlockSpec((cols, step), lambda k, t: (0, k))
    return pl.pallas_call(
        product_kernel,
        grid_spec=pltpu.PrefetchScalarGridSpec(
            num_scalar_prefetch=1,
            grid=(STEPS,),
            in_specs=[pl.BlockSpec((p.shape[0], step), lambda k, t: (0, k)) for p in parts] + [spec_b, spec_b],
            out_specs=pl.BlockSpec((NC, rows, cols), lambda k, t: (0, 0, 0)),
        ),
        out_shape=jax.ShapeDtypeStruct((NC, rows, cols), F32),
        compiler_params=pltpu.CompilerParams(vmem_limit_bytes=54 * 2**20),
        cost_estimate=pl.CostEstimate(
            flops=4 * rows * cols * depth, bytes_accessed=2 * depth * (rows + 2 * cols) + 8 * rows * cols, transcendentals=0
        ),
    )(at, *parts, b, b_other)


def last_kernel(at_ref, x0_ref, x1_ref, load_ref, near_ref, b_ref, b_other_ref, o_ref):
    k, c = pl.program_id(0), at_ref[2]
    n, m = load_ref.shape[1] // NX, near_ref.shape[1] // NX
    x = jnp.concatenate([x0_ref[...], x1_ref[...]], axis=0)
    each = x.shape[0] // NX

    @pl.when(k == 0)
    def _():
        for i in range(NC * NX):
            h, p = i // NX, i % NX
            o_ref[i, :n, :] = load_ref[h, p * n : (p + 1) * n, :]
            o_ref[i, n : n + m, :] = near_ref[h, p * m : (p + 1) * m, :]
            o_ref[i, n + m :, :] = jnp.zeros((each, o_ref.shape[2]), F32)

    for b, h in ((b_ref, c), (b_other_ref, 1 - c)):
        r = lax.dot_general(x, b[...], (((1,), (1,)), ((), ())), preferred_element_type=F32)
        for p in range(NX):
            o_ref[h * NX + p, n + m :, :] += r[p * each : (p + 1) * each, :]


def last_product(at, parts, load, near, b, b_other):
    rows, depth = sum(p.shape[0] for p in parts), parts[0].shape[1]
    cols, step = b.shape[0], depth // STEPS
    total = (rows + load.shape[1] + near.shape[1]) // NX
    spec_b = pl.BlockSpec((cols, step), lambda k, t: (0, k))
    return pl.pallas_call(
        last_kernel,
        grid_spec=pltpu.PrefetchScalarGridSpec(
            num_scalar_prefetch=1,
            grid=(STEPS,),
            in_specs=[pl.BlockSpec((p.shape[0], step), lambda k, t: (0, k)) for p in parts]
            + [pl.BlockSpec(p.shape, lambda k, t: (0, 0, 0)) for p in (load, near)]
            + [spec_b, spec_b],
            out_specs=pl.BlockSpec((NC * NX, total, cols), lambda k, t: (0, 0, 0)),
        ),
        out_shape=jax.ShapeDtypeStruct((NC * NX, total, cols), F32),
        compiler_params=pltpu.CompilerParams(vmem_limit_bytes=54 * 2**20),
        cost_estimate=pl.CostEstimate(
            flops=4 * rows * cols * depth, bytes_accessed=2 * depth * (rows + 2 * cols) + 32 * total * cols, transcendentals=0
        ),
    )(at, *parts, load, near, b, b_other)


def sum_over_x(partial):
    cols = partial.shape[2]
    terms = lax.all_to_all(partial.reshape(-1, cols), ("core", "x"), 0, 0, tiled=True)
    total = terms.reshape(NC, NX, -1, cols).sum(1).astype(BF16)
    return total.reshape(-1, cols)


def finish_kernel(at_ref, g_ref, own_ref, other_ref, o_ref, rows, turned):
    y, z, c = at_ref[0], at_ref[1], at_ref[2]

    @pl.when(pl.program_id(0) == 0)
    def _():
        stride = g_ref.shape[0] // (NX * ROWS)
        one = NZ // NX
        for skip, y_steps in ((0, (0,)), (one, (-1, 1)), (3 * one, (2,))):
            each = len(y_steps) * one
            for j in range(NX * NC * each):
                slot, s = j // (NC * each), (j // each) % NC
                i = slot * stride + s * NY * one + skip + j % each
                block = slot * each + j % each
                y_at = lax.rem(y + (y_steps[block // NZ] + NY), NY)
                z_at = lax.rem(z + (NZ - block % NZ), NZ)
                to = pl.multiple_of(((y_at * NZ + z_at) * NC + s) * ROWS, ROWS)
                rows[pl.ds(to, ROWS), :] = g_ref[i * ROWS : (i + 1) * ROWS, :]
        for e in range(EXAMPLES):
            turned[e] = rows[e * T_EX : (e + 1) * T_EX, :].T

    for i in range(EXAMPLES):
        ref, core = (own_ref, c) if i < NY else (other_ref, 1 - c)
        r = jnp.dot(turned[(i % NY) * NC + core], ref[0, i % NY], preferred_element_type=F32)
        r = r * r
        if i > 0:
            r = r + o_ref[...]
        if i == EXAMPLES - 1:
            r = r * (1.0 / (EXAMPLES * T_EX))
        o_ref[...] = r


def finish(at, g_all, own, other):
    tokens, cols = g_all.shape
    n_blk = own.shape[3]
    spec_a = pl.BlockSpec((1, NY, T_EX, n_blk), lambda j, t: (j, 0, 0, 0))
    return pl.pallas_call(
        finish_kernel,
        grid_spec=pltpu.PrefetchScalarGridSpec(
            num_scalar_prefetch=1,
            grid=(NZ,),
            in_specs=[pl.BlockSpec((tokens, cols), lambda j, t: (0, 0)), spec_a, spec_a],
            out_specs=pl.BlockSpec((cols, n_blk), lambda j, t: (0, j)),
            scratch_shapes=[pltpu.VMEM((tokens, cols), BF16), pltpu.VMEM((EXAMPLES, cols, T_EX), BF16)],
        ),
        out_shape=jax.ShapeDtypeStruct((cols, NZ * n_blk), F32),
        compiler_params=pltpu.CompilerParams(vmem_limit_bytes=24 * 2**20),
        cost_estimate=pl.CostEstimate(
            flops=2 * tokens * cols * NZ * n_blk, bytes_accessed=4 * cols * NZ * n_blk + 4 * tokens * n_blk * NZ, transcendentals=0
        ),
    )(at, g_all, own, other)


def after(values, *others):
    return lax.optimization_barrier((tuple(values), others))[0]


def body(acts, grads, act_basis, grad_basis):
    y, z, c = (lax.axis_index(a) for a in ("y", "z", "core"))
    at = jnp.stack([y, z, c]).astype(jnp.int32)
    basis = grad_basis.T
    basis_other = shift(basis, "core", 1)
    rows = lax.all_gather(acts, "z", axis=1, tiled=True)
    load = jnp.concatenate(ring_z(grads), axis=0)
    h = load.shape[0] // 2

    below, above = shift(load, "y", 1), shift(load, "y", -1)
    product_load = product(at, [load], basis, basis_other)
    (act_basis,) = after([act_basis], product_load)
    basis_acts = lax.all_to_all(act_basis, "z", 1, 0, tiled=True)
    (rows,) = after([rows], load, product_load)
    partial = jnp.dot(rows, basis_acts, preferred_element_type=F32)
    terms = lax.all_to_all(partial, ("y", "core"), 0, 0, tiled=True)
    piece = terms.reshape(NY * NC, T_EX, -1).sum(0).astype(BF16)

    far = [shift(below[:h], "y", 1), shift(above[h:], "y", -1)]
    product_near = product(at, [below, above], basis, basis_other)
    along_y = lax.all_to_all(jnp.broadcast_to(piece[None], (NY,) + piece.shape), "y", 0, 0, tiled=True)
    (along_y,) = after([along_y], product_near, *far)
    own = lax.all_gather(along_y, "z", axis=0)

    far = after(far, product_near, along_y)
    total = sum_over_x(last_product(at, far, product_load, product_near, basis, basis_other))
    (own,) = after([own], total)
    g_all = lax.all_gather(total, "x", axis=0, tiled=True)
    return finish(at, g_all, own, shift(own, "core", 1))


def solution(mesh):
    wide = ("y", "z", "core")
    return jax.shard_map(
        body,
        mesh=Mesh(mesh.devices.reshape(NY, NZ, NC, NX), wide + ("x",)),
        in_specs=(P(None, wide), P(wide, "x"), P(wide, "x"), P("x", wide)),
        out_specs=P(wide, "x"),
        check_vma=False,
    )
```
